128 devices in a mesh: row: 16 (over z, y), col: 8 (over x, core).
Axes of the slice: x: 4, y: 4, z: 4, core: 2. Of those that a mesh axis runs over, the one named last changes fastest.
Arguments:
- child_fronts: float32 [128, 2048, 2048], P(('row', 'col')), may hold values from -3 to 20, as said below
- child_tiles: int32 [128, 12], P(('row', 'col')), may hold values from 0 to 63, as said below
- parent_front: float32 [8192, 8192], P('row', 'col'), may hold values from -5 to 20, as said below
Outputs:
- child_factors: float32 [128, 2048, 512], P(('row', 'col'))
- parent_result: float32 [8192, 8192], P('row', 'col')
The draws below stay inside these ranges and needn't reach their ends.
Inputs may be any that keep to these rules, and one draw needn't show every extreme that they name: `child_tiles`: each row holds strictly increasing parent tile indices, no two of them in the same group of 4 consecutive tiles. `child_fronts`: each child front is symmetric positive definite. `parent_front`: symmetric positive definite.
All inputs are finite; a program needn't handle non-finite values.
Results may differ from the reference program's by a relative error of at most 0.0003.
Values sent between devices are 32-bit elements; how exact they have to be, the bound alone decides.
No kernel may reach another device: no remote copies, remote signals or barrier semaphores. Data moves between devices by JAX's collectives and lax.ppermute only.
A program may use at most 192 MiB of HBM per device.

```python
import math
import jax
import jax.numpy as jnp
from jax import lax

F = 8192
PANEL = 512
TILE = 128
CW = 2048
CP = 512
PANELS = 2
CHILDREN = 128
TPB = 4
NB = 16
CT = 12


MARGIN = 0.05


def grid_front(key, order, weight_lo, weight_hi, noise_scale):
    subkeys = jax.random.split(key, 3)
    cells = jnp.arange(order, dtype=jnp.int32)
    depth = order // 64
    x_pos = cells % 8
    y_pos = cells // 8 % 8
    z_pos = cells // 64
    edges = jax.random.uniform(subkeys[0], (6, order), jnp.float32, weight_lo, weight_hi)
    along_x = edges[0]
    along_y = edges[1]
    along_z = edges[2]
    back_x = jnp.where(x_pos > 0, jnp.roll(along_x, 1), edges[3])
    back_y = jnp.where(y_pos > 0, jnp.roll(along_y, 8), edges[4])
    back_z = jnp.where(z_pos > 0, jnp.roll(along_z, 64), edges[5])
    diagonal = along_x + back_x + along_y + back_y + along_z + back_z + noise_scale * (1.0 + MARGIN)
    rows = cells[:, None]
    cols = cells[None, :]
    gap = cols - rows
    coupling = jnp.where((gap == 1) & (x_pos[:, None] < 7), along_x[:, None], 0.0)
    coupling = coupling + jnp.where((gap == -1) & (x_pos[None, :] < 7), along_x[None, :], 0.0)
    coupling = coupling + jnp.where((gap == 8) & (y_pos[:, None] < 7), along_y[:, None], 0.0)
    coupling = coupling + jnp.where((gap == -8) & (y_pos[None, :] < 7), along_y[None, :], 0.0)
    coupling = coupling + jnp.where((gap == 64) & (z_pos[:, None] < depth - 1), along_z[:, None], 0.0)
    coupling = coupling + jnp.where((gap == -64) & (z_pos[None, :] < depth - 1), along_z[None, :], 0.0)
    order_plus = order + 1
    shuffled = jax.random.permutation(subkeys[1], order).astype(jnp.int32) + 1
    scales = jax.random.uniform(subkeys[2], (order,), jnp.float32, 0.6, 1.0)
    residue = shuffled[:, None] * shuffled[None, :] % (2 * order_plus)
    sine = jnp.sin(residue.astype(jnp.float32) * (math.pi / order_plus)) * math.sqrt(2.0 / order_plus)
    noise = noise_scale * scales[:, None] * scales[None, :] * sine
    return jnp.where(rows == cols, diagonal[:, None], 0.0) - coupling + noise


def block_pairs(key, order, block_width, pair_count):
    cells = jnp.arange(order, dtype=jnp.int32)
    block_of = cells // block_width
    signs = 2.0 * jax.random.randint(key, (2, order), 0, 2).astype(jnp.float32) - 1.0
    low_vec = jnp.where(block_of < pair_count, signs[0], 0.0)
    high_vec = jnp.where((block_of >= 1) & (block_of <= pair_count), signs[1], 0.0)
    same = block_of[:, None] == block_of[None, :]
    term = jnp.where(same, low_vec[:, None] * low_vec[None, :] + high_vec[:, None] * high_vec[None, :], 0.0)
    term = term + jnp.where(block_of[None, :] == block_of[:, None] + 1, low_vec[:, None] * high_vec[None, :], 0.0)
    term = term + jnp.where(block_of[:, None] == block_of[None, :] + 1, high_vec[:, None] * low_vec[None, :], 0.0)
    return term


def draw_child_fronts(key, part):
    subkeys = jax.random.split(key, CHILDREN)
    return lax.map(lambda single: grid_front(single, CW, 0.5, 1.5, 6.0), subkeys)


def draw_parent_front(key, part):
    pair_key = jax.random.fold_in(key, 7)
    coupled = block_pairs(pair_key, F, PANEL, PANELS)
    return grid_front(key, F, 0.5, 1.5, 6.0) + coupled


def draw_child_tiles(key, part):
    subkeys = jax.random.split(key, CHILDREN + 1)
    orders = jax.vmap(lambda single: jax.random.permutation(single, NB))(subkeys[:CHILDREN]).astype(jnp.int32)
    block_ids = jnp.arange(NB, dtype=jnp.int32)
    favour = jnp.where((block_ids == 0) | (block_ids == NB - 1), NB, 0).astype(jnp.int32)
    first_child = (jnp.arange(CHILDREN, dtype=jnp.int32) == 0)[:, None]
    scores = orders + jnp.where(first_child, favour[None, :], 0)
    chosen = jax.lax.top_k(scores, CT)[1]
    blocks_sorted = jnp.sort(chosen, axis=1).astype(jnp.int32)
    offsets = jax.random.randint(subkeys[CHILDREN], (CHILDREN, CT), 0, TPB).astype(jnp.int32)
    position = jnp.arange(CT, dtype=jnp.int32)[None, :]
    offsets = jnp.where(first_child & (position == 0), 0, offsets)
    offsets = jnp.where(first_child & (position == CT - 1), TPB - 1, offsets)
    return (blocks_sorted * TPB + offsets).astype(jnp.int32)


def setup_inputs(seed: int = 0) -> dict:
    keys = jax.random.split(jax.random.key(seed), 4)
    return {
        "child_fronts": draw_child_fronts(jax.random.fold_in(keys[3], 71), 0),
        "child_tiles": draw_child_tiles(jax.random.fold_in(keys[3], 71), 0),
        "parent_front": draw_parent_front(jax.random.fold_in(keys[3], 71), 0),
    }


PRECISE = lax.Precision.HIGHEST

def product(left_side, right_side):
    return lax.dot_general(left_side.astype(jnp.float32), right_side.astype(jnp.float32), (((1,), (1,)), ((), ())), precision=PRECISE, preferred_element_type=jnp.float32)

def right_solve(factor, right_block):
    return jax.scipy.linalg.solve_triangular(factor, right_block.T, lower=True).T

def eliminate_child(matrix):
    corner = jnp.linalg.cholesky(matrix[:CP, :CP])
    below_rows = right_solve(corner, matrix[CP:, :CP])
    update = matrix[CP:, CP:] - product(below_rows, below_rows)
    return (jnp.concatenate([corner, below_rows], axis=0), update)

def reference(child_fronts, child_tiles, parent_front):
    offsets = jnp.arange(TILE, dtype=jnp.int32)

    def absorb(assembled, element):
        matrix, indices = element
        factor, update = eliminate_child(matrix)
        rows_all = (indices[:, None] * TILE + offsets[None, :]).reshape(-1).astype(jnp.int32)
        assembled = assembled.at[rows_all[:, None], rows_all[None, :]].add(update)
        return (assembled, factor)
    assembled, factors = lax.scan(absorb, parent_front, (child_fronts, child_tiles))
    for pivot_step in range(PANELS):
        first_row = pivot_step * PANEL
        after_row = first_row + PANEL
        corner = jnp.linalg.cholesky(assembled[first_row:after_row, first_row:after_row])
        below_rows = right_solve(corner, assembled[after_row:, first_row:after_row])
        trailing = assembled[after_row:, after_row:] - product(below_rows, below_rows)
        column_block = jnp.concatenate([jnp.zeros((first_row, PANEL), jnp.float32), corner, below_rows], axis=0)
        assembled = assembled.at[after_row:, after_row:].set(trailing)
        assembled = assembled.at[first_row:after_row, after_row:].set(0.0)
        assembled = assembled.at[:, first_row:after_row].set(column_block)
    return (factors, assembled)
```

```python
import functools

import jax
import jax.numpy as jnp
from jax import lax
from jax.experimental import pallas as pl
from jax.experimental.pallas import tpu as pltpu
from jax.sharding import PartitionSpec as P

PANEL = 512
TILE = 128
CP = 512
CW = 2048
CT = 12
REST = CW - CP
PIV = 1024
DEV = 128
PAIRS = CT * (CT + 1) // 2
SLOTS = 80
META = PAIRS
AXES = ("row", "col")
PRECISE = lax.Precision.HIGHEST
VMEM = 56 * 1024 * 1024

pair_slot = {}
for _i in range(CT):
    for _j in range(_i + 1):
        pair_slot[_i, _j] = len(pair_slot)

corner_slot = {}
for _i in range(8):
    for _j in range(_i + 1):
        corner_slot[_i, _j] = len(corner_slot)
CORNER = 40
BACK = 128


def dot_t(x, y):
    return lax.dot_general(
        x, y, (((1,), (1,)), ((), ())), precision=PRECISE, preferred_element_type=jnp.float32
    )


def split(x):
    high = x.astype(jnp.bfloat16)
    return high, (x - high.astype(jnp.float32)).astype(jnp.bfloat16)


def dot_split(x, y):
    dims = (((1,), (1,)), ((), ()))
    f = functools.partial(lax.dot_general, dimension_numbers=dims, preferred_element_type=jnp.float32)
    return f(x[0], y[0]) + (f(x[0], y[1]) + f(x[1], y[0]))


def inverse_factor(tile):
    shape = (8, TILE)
    lane = lax.broadcasted_iota(jnp.int32, shape, 1)
    sub = lax.broadcasted_iota(jnp.int32, shape, 0)
    full = lambda v: jnp.broadcast_to(v, shape)
    rows = [tile[8 * k : 8 * k + 8, :] for k in range(16)]
    out = []
    for k in range(16):
        base = 8 * k
        columns = [[full(rows[q][:, base + m : base + m + 1]) for m in range(8)] for q in range(k, 16)]
        a = [[full(columns[0][n][m : m + 1, :]) if n >= m else None for n in range(8)] for m in range(8)]
        inside = (lane >= base) & (lane < base + 8)
        own = jnp.where(inside, jnp.where(lane - base == sub, 1.0, 0.0), rows[k])
        v = [full(own[m : m + 1, :]) for m in range(8)]
        w = []
        for m in range(8):
            r = 1.0 / a[m][m]
            g = [a[m][n] * r if n > m else None for n in range(8)]
            for n in range(m + 1, 8):
                for p in range(n, 8):
                    a[n][p] = a[n][p] - g[n] * a[m][p]
            for n in range(m + 1, 8):
                v[n] = v[n] - g[n] * v[m]
            w.append(v[m] * r)
            for q in range(1, 16 - k):
                for n in range(m + 1, 8):
                    columns[q][n] = columns[q][n] - columns[q][m] * g[n]
        for q in range(1, 16 - k):
            terms = [columns[q][m] * w[m] for m in range(8)]
            while len(terms) > 1:
                terms = [terms[t] + terms[t + 1] for t in range(0, len(terms), 2)]
            rows[k + q] = jnp.where(inside, 0.0, rows[k + q]) - terms[0]
        mine, scale = v[0], a[0][0]
        for m in range(1, 8):
            mine = jnp.where(sub == m, v[m], mine)
            scale = jnp.where(sub == m, a[m][m], scale)
        out.append(jnp.where(lane <= base + sub, mine * lax.rsqrt(scale), 0.0))
    return jnp.concatenate(out, axis=0)


def factor_blocks(a_ref, l_ref, inv_ref, order):
    count = order // TILE
    tri = lax.broadcasted_iota(jnp.int32, (TILE, TILE), 0) >= lax.broadcasted_iota(
        jnp.int32, (TILE, TILE), 1
    )

    def step(kb, _):
        at = pl.multiple_of(kb * TILE, TILE)
        inverse = inverse_factor(a_ref[pl.ds(at, TILE), pl.ds(at, TILE)])
        inv_ref[pl.ds(at, TILE), :] = inverse
        for q in range(count):

            @pl.when(kb == q)
            def _():
                lo = q * TILE
                panel = dot_t(a_ref[lo:order, lo : lo + TILE], inv_ref[lo : lo + TILE, :])
                l_ref[lo : lo + TILE, lo : lo + TILE] = jnp.where(tri, panel[:TILE], 0.0)
                if q + 1 < count:
                    l_ref[lo + TILE : order, lo : lo + TILE] = panel[TILE:]
                    for j in range(q + 1, count):
                        left = panel[(j - q) * TILE :]
                        a_ref[j * TILE : order, j * TILE : (j + 1) * TILE] = a_ref[
                            j * TILE : order, j * TILE : (j + 1) * TILE
                        ] - dot_t(left, left[:TILE])

        return 0

    lax.fori_loop(0, count, step, 0)


def child_kernel(tiles_ref, front_ref, factor_ref, out_ref, a_ref, b_ref, c_ref, inv_ref, hi_ref, lo_ref, sems):
    copy_a = pltpu.make_async_copy(front_ref.at[pl.ds(0, CP), pl.ds(0, CP)], a_ref, sems.at[0])
    copy_b = pltpu.make_async_copy(front_ref.at[pl.ds(CP, REST), pl.ds(0, CP)], b_ref, sems.at[1])
    copy_c = pltpu.make_async_copy(front_ref.at[pl.ds(CP, REST), pl.ds(CP, REST)], c_ref, sems.at[2])
    copy_a.start()
    copy_b.start()
    copy_c.start()
    copy_a.wait()
    factor_ref[0:CP, :] = jnp.zeros((CP, CP), jnp.float32)
    factor_blocks(a_ref, factor_ref, inv_ref, CP)
    copy_b.wait()
    for kb in range(CP // TILE):
        lo = kb * TILE
        part = b_ref[:, lo : lo + TILE]
        if kb:
            part = part - dot_split(
                (hi_ref[:, :lo], lo_ref[:, :lo]), split(factor_ref[lo : lo + TILE, :lo])
            )
        part = dot_t(part, inv_ref[lo : lo + TILE, :])
        factor_ref[CP:CW, lo : lo + TILE] = part
        high, low = split(part)
        hi_ref[:, lo : lo + TILE] = high
        lo_ref[:, lo : lo + TILE] = low
    copy_c.wait()
    for i in range(CT):
        rows = slice(i * TILE, (i + 1) * TILE)
        wide = (i + 1) * TILE
        update = c_ref[rows, :wide] - dot_split(
            (hi_ref[rows, :], lo_ref[rows, :]), (hi_ref[:wide, :], lo_ref[:wide, :])
        )
        for j in range(i + 1):
            out_ref[pl.ds(pair_slot[i, j], DEV, stride=SLOTS), :] = update[:, j * TILE : (j + 1) * TILE]
    meta = jnp.broadcast_to(tiles_ref[0:1, :], (DEV, TILE))
    out_ref[pl.ds(META, DEV, stride=SLOTS), :] = meta
    out_ref[pl.ds(META + 1, DEV, stride=SLOTS), :] = meta


def eliminate_child(front, tiles):
    spec = pl.BlockSpec(memory_space=pltpu.VMEM)
    return pl.pallas_call(
        child_kernel,
        out_shape=(
            jax.ShapeDtypeStruct((CW, CP), jnp.float32),
            jax.ShapeDtypeStruct((DEV * SLOTS, TILE), jnp.float32),
        ),
        in_specs=[spec, pl.BlockSpec(memory_space=pl.ANY)],
        out_specs=(spec, spec),
        scratch_shapes=[
            pltpu.VMEM((CP, CP), jnp.float32),
            pltpu.VMEM((REST, CP), jnp.float32),
            pltpu.VMEM((REST, REST), jnp.float32),
            pltpu.VMEM((CP, TILE), jnp.float32),
            pltpu.VMEM((REST, CP), jnp.bfloat16),
            pltpu.VMEM((REST, CP), jnp.bfloat16),
            pltpu.SemaphoreType.DMA((3,)),
        ],
        compiler_params=pltpu.CompilerParams(vmem_limit_bytes=VMEM),
        cost_estimate=pl.CostEstimate(flops=12 * 10**9, bytes_accessed=30 * 10**6, transcendentals=0),
        name="child",
    )(tiles, front)


def sum_kernel(parent_ref, in_ref, corner_ref, back_ref, acc_ref, meta_ref, pack_ref, table_ref, sem):
    acc_ref[0 : DEV * 32, :] = parent_ref[...]
    ids = in_ref[pl.ds(META, DEV, stride=SLOTS), :].astype(jnp.int32)
    as_row = (ids // 4) * 256 + (ids % 4) * 8
    as_col = (ids // 8) * 32 + ids % 8
    lane = lax.broadcasted_iota(jnp.int32, (DEV, TILE), 1)
    meta_ref[...] = jnp.where(lane < 64, as_row, pltpu.roll(as_col, 64, axis=1))
    copy = pltpu.make_async_copy(meta_ref, table_ref, sem)
    copy.start()
    copy.wait()

    def add_child(s, _):
        base = s * SLOTS
        row_of = [table_ref[s, i] for i in range(CT)]
        col_of = [table_ref[s, 64 + j] for j in range(CT)]
        todo = list(pair_slot.items())
        for first in range(0, PAIRS, 26):
            group = todo[first : first + 26]
            places = [row_of[i] + col_of[j] for (i, j), _ in group]
            sums = [
                acc_ref[pl.ds(place, 1), :] + in_ref[pl.ds(base + slot, 1), :]
                for place, (_, slot) in zip(places, group)
            ]
            for place, total in zip(places, sums):
                acc_ref[pl.ds(place, 1), :] = total
        return 0

    lax.fori_loop(0, DEV, add_child, 0)

    for (i, j), slot in corner_slot.items():
        place = (i // 4) * 256 + (i % 4) * 8 + j
        pack_ref[slot : slot + 1, :] = acc_ref[place : place + 1, :]
    for slot in range(len(corner_slot), CORNER):
        pack_ref[slot : slot + 1, :] = jnp.zeros((1, TILE), jnp.float32)
    pack = pack_ref[...]
    sub = lax.broadcasted_iota(jnp.int32, (8, TILE), 0)

    def pack_device(g, _):
        corner_ref[pl.ds(pl.multiple_of(g * CORNER, 8), CORNER), :] = pack
        r = g // 8
        c = g % 8
        base = pl.multiple_of(g * BACK, 8)
        odd = (r % 2) == 1
        first = jnp.where(sub < 4, 0, 1) + 2 * c <= r
        for k in range(4):
            lower = acc_ref[pl.ds(pl.multiple_of(g * 32 + k * 8, 8), 8), :]
            m0 = acc_ref[pl.ds(pl.multiple_of(((2 * c) * 8 + r // 2) * 32 + k * 8, 8), 8), :]
            m1 = acc_ref[pl.ds(pl.multiple_of(((2 * c + 1) * 8 + r // 2) * 32 + k * 8, 8), 8), :]
            m0 = jnp.where(odd, pltpu.roll(m0, 4, axis=0), m0)
            m1 = jnp.where(odd, m1, pltpu.roll(m1, 4, axis=0))
            upper = jnp.where(sub < 4, m0, m1)
            back_ref[pl.ds(base + k * 8, 8), :] = jnp.where(first, lower, upper)
        back_ref[pl.ds(base + 32, 32), :] = acc_ref[pl.ds(pl.multiple_of(r * 256, 8), 32), :]
        back_ref[pl.ds(base + 64, 32), :] = acc_ref[pl.ds(pl.multiple_of(c * 512, 8), 32), :]
        back_ref[pl.ds(base + 96, 32), :] = acc_ref[pl.ds(pl.multiple_of(c * 512 + 256, 8), 32), :]
        return 0

    lax.fori_loop(0, DEV, pack_device, 0)


def sum_slices(parent, arrived):
    spec = pl.BlockSpec(memory_space=pltpu.VMEM)
    return pl.pallas_call(
        sum_kernel,
        out_shape=(
            jax.ShapeDtypeStruct((DEV * CORNER, TILE), jnp.float32),
            jax.ShapeDtypeStruct((DEV * BACK, TILE), jnp.float32),
        ),
        in_specs=[spec, spec],
        out_specs=(spec, spec),
        scratch_shapes=[
            pltpu.VMEM((DEV * 32, TILE), jnp.float32),
            pltpu.VMEM((DEV, TILE), jnp.int32),
            pltpu.VMEM((CORNER, TILE), jnp.float32),
            pltpu.SMEM((DEV, TILE), jnp.int32),
            pltpu.SemaphoreType.DMA,
        ],
        compiler_params=pltpu.CompilerParams(vmem_limit_bytes=VMEM),
        name="sum_slices",
    )(parent, arrived)


def corner_kernel(in_ref, l_ref, inv_ref, a_ref):
    for (i, j), slot in corner_slot.items():
        a_ref[i * TILE : (i + 1) * TILE, j * TILE : (j + 1) * TILE] = in_ref[
            pl.ds(slot, DEV, stride=CORNER), :
        ]
    l_ref[...] = jnp.zeros((PIV, PIV), jnp.float32)
    factor_blocks(a_ref, l_ref, inv_ref, PIV)


def factor_corner(arrived):
    spec = pl.BlockSpec(memory_space=pltpu.VMEM)
    return pl.pallas_call(
        corner_kernel,
        out_shape=(
            jax.ShapeDtypeStruct((PIV, PIV), jnp.float32),
            jax.ShapeDtypeStruct((PIV, TILE), jnp.float32),
        ),
        in_specs=[spec],
        out_specs=(spec, spec),
        scratch_shapes=[pltpu.VMEM((PIV, PIV), jnp.float32)],
        compiler_params=pltpu.CompilerParams(vmem_limit_bytes=VMEM),
        cost_estimate=pl.CostEstimate(flops=70 * 10**9, bytes_accessed=10**7, transcendentals=0),
        name="corner",
    )(arrived)


def finish_kernel(where_ref, in_ref, l_ref, inv_ref, out_ref, x_ref, hi_ref, lo_ref):
    r = where_ref[0]
    c = where_ref[1]
    tile = lambda slot: in_ref[pl.ds(slot, DEV, stride=BACK), :]
    rows = 3 * PANEL

    @pl.when(r >= 2)
    def _():
        for a in range(CT):
            for j in range(8):
                x_ref[a * TILE : (a + 1) * TILE, j * TILE : (j + 1) * TILE] = tile(32 + a * 8 + j)
        for kb in range(PIV // TILE):
            lo = kb * TILE
            part = x_ref[:, lo : lo + TILE]
            if kb:
                part = part - dot_split(
                    (hi_ref[:, :lo], lo_ref[:, :lo]), split(l_ref[lo : lo + TILE, :lo])
                )
            part = dot_t(part, inv_ref[lo : lo + TILE, :])
            x_ref[:, lo : lo + TILE] = part
            high, low = split(part)
            hi_ref[:, lo : lo + TILE] = high
            lo_ref[:, lo : lo + TILE] = low

    @pl.when((r >= 2) & (c >= 1))
    def _():
        for q in range(2):
            cols = slice(PANEL * (q + 1), PANEL * (q + 2))
            out_ref[:, q * PANEL : (q + 1) * PANEL] = dot_split(
                (hi_ref[:PANEL, :], lo_ref[:PANEL, :]), (hi_ref[cols, :], lo_ref[cols, :])
            )
            for a in range(4):
                for b in range(4):
                    spot = (slice(a * TILE, (a + 1) * TILE), slice(q * PANEL + b * TILE, q * PANEL + (b + 1) * TILE))
                    mirrored = (r < 2 * c + q) | ((r == 2 * c + q) & (a < b))

                    @pl.when(mirrored)
                    def _():
                        out_ref[spot] = tile(b * 8 + q * 4 + a).T - out_ref[spot]

                    @pl.when(jnp.logical_not(mirrored))
                    def _():
                        out_ref[spot] = tile(a * 8 + q * 4 + b) - out_ref[spot]

    @pl.when((r >= 2) & (c == 0))
    def _():
        out_ref[...] = x_ref[:PANEL, :]

    @pl.when((r < 2) & (c == 0))
    def _():
        out_ref[...] = l_ref[pl.ds(pl.multiple_of(r * PANEL, PANEL), PANEL), :]

    @pl.when((r < 2) & (c >= 1))
    def _():
        out_ref[...] = jnp.zeros((PANEL, PIV), jnp.float32)


def finish(where, arrived, corner, inverses):
    spec = pl.BlockSpec(memory_space=pltpu.VMEM)
    rows = 3 * PANEL
    return pl.pallas_call(
        finish_kernel,
        out_shape=jax.ShapeDtypeStruct((PANEL, PIV), jnp.float32),
        in_specs=[pl.BlockSpec(memory_space=pltpu.SMEM), spec, spec, spec],
        out_specs=spec,
        scratch_shapes=[
            pltpu.VMEM((rows, PIV), jnp.float32),
            pltpu.VMEM((rows, PIV), jnp.bfloat16),
            pltpu.VMEM((rows, PIV), jnp.bfloat16),
        ],
        compiler_params=pltpu.CompilerParams(vmem_limit_bytes=VMEM),
        name="finish",
    )(where, arrived, corner, inverses)


def exchange(x):
    y = x.reshape(DEV, x.shape[0] // DEV, TILE)
    return lax.all_to_all(y, AXES, 0, 0, tiled=True).reshape(x.shape)


def on_device(child_fronts, child_tiles, parent_front):
    row = lax.axis_index("row")
    col = lax.axis_index("col")
    parent = parent_front.reshape(4, TILE, 8, TILE).transpose(1, 0, 2, 3).reshape(DEV * 32, TILE)
    parent = exchange(parent)
    tiles = jnp.pad(child_tiles.astype(jnp.float32), ((0, 7), (0, TILE - CT)))
    factor, outgoing = eliminate_child(child_fronts[0], tiles)
    corner_rows, back_rows = sum_slices(parent, exchange(outgoing))
    corner, inverses = factor_corner(exchange(corner_rows))
    where = jnp.stack([row, col]).astype(jnp.int32)
    result = finish(where, exchange(back_rows), corner, inverses)
    return factor[None], result


def solution(mesh):
    placed = (P(AXES, None, None), P(AXES, None), P("row", "col"))
    return jax.shard_map(
        on_device,
        mesh=mesh,
        in_specs=placed,
        out_specs=(P(AXES, None, None), P("row", "col")),
        check_vma=False,
    )
```

```python
import functools

import jax
import jax.numpy as jnp
from jax import lax
from jax.experimental import pallas as pl
from jax.experimental.pallas import tpu as pltpu
from jax.sharding import PartitionSpec as P

PANEL = 512
TILE = 128
CP = 512
CW = 2048
CT = 12
REST = CW - CP
PIV = 1024
DEV = 128
PAIRS = CT * (CT + 1) // 2
AXES = ("row", "col")
PRECISE = lax.Precision.HIGHEST
VMEM = 56 * 1024 * 1024

SLOTS = 80
META = PAIRS
CHUNKS = 4

pair_slot = {}
for _i in range(CT):
    for _j in range(_i + 1):
        pair_slot[_i, _j] = len(pair_slot)

corner_slot = {}
for _i in range(8):
    for _j in range(_i + 1):
        corner_slot[_i, _j] = len(corner_slot)
HALF = 24
BACK = 80
BLOCK = 32
WIDE = 2 * TILE


def dot_t(x, y):
    return lax.dot_general(
        x, y, (((1,), (1,)), ((), ())), precision=PRECISE, preferred_element_type=jnp.float32
    )


def dot(x, y):
    return lax.dot_general(
        x, y, (((1,), (0,)), ((), ())), precision=PRECISE, preferred_element_type=jnp.float32
    )


def split(x):
    high = x.astype(jnp.bfloat16)
    return high, (x - high.astype(jnp.float32)).astype(jnp.bfloat16)


def dot_split(x, y):
    dims = (((1,), (1,)), ((), ()))
    f = functools.partial(lax.dot_general, dimension_numbers=dims, preferred_element_type=jnp.float32)
    return f(x[0], y[0]) + (f(x[0], y[1]) + f(x[1], y[0]))


def total(terms):
    while len(terms) > 1:
        terms = [terms[t] + terms[t + 1] for t in range(0, len(terms), 2)]
    return terms[0]


SPREAD = 256


def inverse_factor(tile, s_ref):
    shape = (8, TILE)
    lane = lax.broadcasted_iota(jnp.int32, shape, 1)
    sub = lax.broadcasted_iota(jnp.int32, shape, 0)
    column = lambda row, at: jnp.broadcast_to(row[:, at : at + 1], shape)
    spread = lambda at: s_ref[pl.ds(at, 8, stride=0), :]
    rows = [tile[8 * k : 8 * k + 8, :] for k in range(16)]
    out = []
    first = [column(rows[0], m) for m in range(8)]
    for k in range(16):
        base = 8 * k
        at = (k % 2) * 72
        columns = [first] + [[column(rows[q], base + m) for m in range(8)] for q in range(k + 1, 16)]
        if k < 15:
            first = [column(rows[k + 1], base + 8 + m) for m in range(8)]
        inside = (lane >= base) & (lane < base + 8)
        for m in range(8):
            s_ref[at + 8 * m : at + 8 * m + 8, :] = columns[0][m]
        s_ref[at + 64 : at + 72, :] = jnp.where(
            inside, jnp.where(lane - base == sub, 1.0, 0.0), rows[k]
        )
        v = [spread(at + 64 + m) for m in range(8)]
        a = [[spread(at + 8 * n + m) if n >= m else None for n in range(8)] for m in range(8)]
        w = []
        inverses = []
        for m in range(8):
            r = 1.0 / a[m][m]
            inverses.append(r)
            g = [a[m][n] * r if n > m else None for n in range(8)]
            for n in range(m + 1, 8):
                for p in range(n, 8):
                    a[n][p] = a[n][p] - g[n] * a[m][p]
            for n in range(m + 1, 8):
                v[n] = v[n] - g[n] * v[m]
            w.append(v[m] * r)
            for q in range(1, 16 - k):
                for n in range(m + 1, 8):
                    columns[q][n] = columns[q][n] - columns[q][m] * g[n]
        if k < 15:
            for m in range(8):
                s_ref[144 + 8 * m : 152 + 8 * m, :] = columns[1][m] * inverses[m]
            for n in range(8):
                first[n] = first[n] - total([columns[1][m] * spread(144 + 8 * m + n) for m in range(8)])
        for q in range(1, 16 - k):
            rows[k + q] = jnp.where(inside, 0.0, rows[k + q]) - total(
                [columns[q][m] * w[m] for m in range(8)]
            )
        mine, scale = v[0], a[0][0]
        for m in range(1, 8):
            mine = jnp.where(sub == m, v[m], mine)
            scale = jnp.where(sub == m, a[m][m], scale)
        out.append(jnp.where(lane <= base + sub, mine * lax.rsqrt(scale), 0.0))
    return jnp.concatenate(out, axis=0)


def factor_blocks(a_ref, l_ref, inv_ref, s_ref, first, last, order):
    count = order // TILE
    tri = lax.broadcasted_iota(jnp.int32, (TILE, TILE), 0) >= lax.broadcasted_iota(
        jnp.int32, (TILE, TILE), 1
    )

    def step(kb, _):
        at = pl.multiple_of(kb * TILE, TILE)
        inverse = inverse_factor(a_ref[pl.ds(at, TILE), pl.ds(at, TILE)], s_ref)
        inv_ref[pl.ds(at, TILE), pl.ds(pl.multiple_of((kb % 2) * TILE, TILE), TILE)] = inverse
        for q in range(first, last):

            @pl.when(kb == q)
            def _():
                lo = q * TILE
                half = q % 2 * TILE
                inverse = inv_ref[lo : lo + TILE, half : half + TILE]
                panel = dot_t(a_ref[lo:order, lo : lo + TILE], inverse)
                l_ref[lo : lo + TILE, lo : lo + TILE] = jnp.where(tri, panel[:TILE], 0.0)
                if q + 1 < count:
                    l_ref[lo + TILE : order, lo : lo + TILE] = panel[TILE:]
                    for j in range(q + 1, count):
                        left = panel[(j - q) * TILE :]
                        a_ref[j * TILE : order, j * TILE : (j + 1) * TILE] = a_ref[
                            j * TILE : order, j * TILE : (j + 1) * TILE
                        ] - dot_t(left, left[:TILE])
                if half:
                    up = inv_ref[lo - TILE : lo, :TILE]
                    inv_ref[lo - TILE : lo, TILE:] = jnp.zeros((TILE, TILE), jnp.float32)
                    inv_ref[lo : lo + TILE, :TILE] = -dot(
                        inverse, dot(l_ref[lo : lo + TILE, lo - TILE : lo], up)
                    )

        return 0

    lax.fori_loop(first, last, step, 0)


def solve_rows(x_ref, hi_ref, lo_ref, l_ref, inv_ref, order):
    for p in range(order // WIDE):
        lo = p * WIDE
        now = slice(lo, lo + WIDE)
        part = x_ref[:, now]
        if p:
            part = part - dot_split((hi_ref[:, :lo], lo_ref[:, :lo]), split(l_ref[now, :lo]))
        part = dot_split(split(part), split(inv_ref[now, :]))
        x_ref[:, now] = part
        hi_ref[:, now], lo_ref[:, now] = split(part)


def child_kernel(tiles_ref, front_ref, factor_ref, out_ref, a_ref, b_ref, c_ref, inv_ref, s_ref, hi_ref, lo_ref, sems):
    copy_a = pltpu.make_async_copy(front_ref.at[pl.ds(0, CP), pl.ds(0, CP)], a_ref, sems.at[0])
    copy_b = pltpu.make_async_copy(front_ref.at[pl.ds(CP, REST), pl.ds(0, CP)], b_ref, sems.at[1])
    copy_c = pltpu.make_async_copy(front_ref.at[pl.ds(CP, REST), pl.ds(CP, REST)], c_ref, sems.at[2])
    copy_a.start()
    copy_b.start()
    copy_c.start()
    copy_a.wait()
    factor_ref[0:CP, :] = jnp.zeros((CP, CP), jnp.float32)
    factor_blocks(a_ref, factor_ref, inv_ref, s_ref, 0, CP // TILE, CP)
    copy_b.wait()
    solve_rows(b_ref, hi_ref, lo_ref, factor_ref, inv_ref, CP)
    factor_ref[CP:CW, :] = b_ref[...]
    copy_c.wait()
    for first in range(0, REST, WIDE):
        rows = slice(first, first + WIDE)
        wide = first + WIDE
        update = c_ref[rows, :wide] - dot_split(
            (hi_ref[rows, :], lo_ref[rows, :]), (hi_ref[:wide, :], lo_ref[:wide, :])
        )
        for k in range(2):
            i = first // TILE + k
            for j in range(i + 1):
                part = update[k * TILE : (k + 1) * TILE, j * TILE : (j + 1) * TILE]
                out_ref[pl.ds(pair_slot[i, j], DEV, stride=SLOTS), :] = part
    meta = jnp.broadcast_to(tiles_ref[0:1, :], (DEV, TILE))
    out_ref[pl.ds(META, DEV, stride=SLOTS), :] = meta
    out_ref[pl.ds(META + 1, DEV, stride=SLOTS), :] = meta


IN_VMEM = pl.BlockSpec(memory_space=pltpu.VMEM)
ANYWHERE = pl.BlockSpec(memory_space=pl.ANY)
IN_SMEM = pl.BlockSpec(memory_space=pltpu.SMEM)
PARAMS = pltpu.CompilerParams(vmem_limit_bytes=VMEM)


def cost(us):
    return pl.CostEstimate(flops=int(us * 10**9), bytes_accessed=int(us * 10**6), transcendentals=0)


def array(rows, columns=TILE, dtype=jnp.float32):
    return jax.ShapeDtypeStruct((rows, columns), dtype)


def eliminate_child(front, tiles):
    return pl.pallas_call(
        child_kernel,
        out_shape=(array(CW, CP), array(DEV * SLOTS)),
        in_specs=[IN_VMEM, ANYWHERE],
        out_specs=(IN_VMEM, IN_VMEM),
        scratch_shapes=[
            pltpu.VMEM((CP, CP), jnp.float32),
            pltpu.VMEM((REST, CP), jnp.float32),
            pltpu.VMEM((REST, REST), jnp.float32),
            pltpu.VMEM((CP, WIDE), jnp.float32),
            pltpu.VMEM((SPREAD, TILE), jnp.float32),
            pltpu.VMEM((REST, CP), jnp.bfloat16),
            pltpu.VMEM((REST, CP), jnp.bfloat16),
            pltpu.SemaphoreType.DMA((3,)),
        ],
        compiler_params=PARAMS,
        cost_estimate=cost(40),
        name="child",
    )(tiles, front)


def sum_kernel(meta_in_ref, parent_ref, in_ref, acc_ref, corner_ref, rows_ref, places_ref, pack_ref, table_ref, sems):
    piece = DEV * SLOTS // CHUNKS
    chunk = lambda k: pltpu.make_async_copy(
        in_ref.at[pl.ds(k * piece, piece)], rows_ref.at[pl.ds(k * piece, piece)], sems.at[k]
    )
    start = pltpu.make_async_copy(parent_ref, acc_ref, sems.at[CHUNKS])
    start.start()
    for k in range(CHUNKS):
        chunk(k).start()
    ids = meta_in_ref[pl.ds(META % 8, DEV, stride=8), :].astype(jnp.int32)
    as_row = (ids // 4) * 256 + (ids % 4) * 8
    as_col = (ids // 8) * 32 + ids % 8
    lane = lax.broadcasted_iota(jnp.int32, (DEV, TILE), 1)
    places_ref[...] = jnp.where(lane < 64, as_row, pltpu.roll(as_col, 64, axis=1))
    table = pltpu.make_async_copy(places_ref, table_ref, sems.at[CHUNKS + 1])
    table.start()
    table.wait()
    start.wait()
    todo = list(pair_slot.items())

    def add_child(s, _):
        base = s * SLOTS
        row_of = [table_ref[s, i] for i in range(CT)]
        col_of = [table_ref[s, 64 + j] for j in range(CT)]
        for first in range(0, len(todo), 26):
            group = todo[first : first + 26]
            places = [row_of[i] + col_of[j] for (i, j), _ in group]
            sums = [
                acc_ref[pl.ds(place, 1), :] + rows_ref[pl.ds(base + slot, 1), :]
                for place, (_, slot) in zip(places, group)
            ]
            for place, total in zip(places, sums):
                acc_ref[pl.ds(place, 1), :] = total
        return 0

    for k in range(CHUNKS):
        chunk(k).wait()
        lax.fori_loop(k * DEV // CHUNKS, (k + 1) * DEV // CHUNKS, add_child, 0)

    for (i, j), slot in corner_slot.items():
        place = (i // 4) * 256 + (i % 4) * 8 + j
        pack_ref[slot : slot + 1, :] = acc_ref[place : place + 1, :]
    pack_ref[len(corner_slot) : 2 * HALF, :] = jnp.zeros((2 * HALF - len(corner_slot), TILE), jnp.float32)

    def send(g, _):
        pltpu.make_async_copy(
            pack_ref.at[pl.ds(pl.multiple_of((g % 2) * HALF, 8), HALF)],
            corner_ref.at[pl.ds(pl.multiple_of(g * HALF, 8), HALF)],
            sems.at[0],
        ).start()
        return 0

    lax.fori_loop(0, DEV, send, 0)
    pltpu.make_async_copy(corner_ref, corner_ref, sems.at[0]).wait()


def sum_slices(parent, arrived):
    return pl.pallas_call(
        sum_kernel,
        grid=(1,),
        out_shape=(array(DEV * 32), array(DEV * HALF)),
        in_specs=[pl.BlockSpec((DEV * 8, TILE), lambda i: (0, 0)), ANYWHERE, ANYWHERE],
        out_specs=(IN_VMEM, ANYWHERE),
        scratch_shapes=[
            pltpu.VMEM((DEV * SLOTS, TILE), jnp.float32),
            pltpu.VMEM((DEV, TILE), jnp.int32),
            pltpu.VMEM((2 * HALF, TILE), jnp.float32),
            pltpu.SMEM((DEV, TILE), jnp.int32),
            pltpu.SemaphoreType.DMA((CHUNKS + 2,)),
        ],
        compiler_params=PARAMS,
        cost_estimate=cost(15),
        name="sum_slices",
    )(arrived.reshape(DEV, SLOTS, TILE)[:, META // 8 * 8 :, :].reshape(DEV * 8, TILE), parent, arrived)


def pack_kernel(acc_ref, back_ref, block_ref, sem):
    sub = lax.broadcasted_iota(jnp.int32, (8, TILE), 0)

    def pack_device(g, _):
        r = g // 8
        c = g % 8
        base = pl.multiple_of(g * BACK, 8)
        for at, place, rows in (
            (0, r * 256 + (c % 2) * 16, 16),
            (16, c * 512, 32),
            (48, c * 512 + 256, 32),
        ):
            pltpu.make_async_copy(
                acc_ref.at[pl.ds(pl.multiple_of(place, 8), rows)],
                back_ref.at[pl.ds(pl.multiple_of(base + at, 8), rows)],
                sem,
            ).start()
        odd = (r % 2) == 1
        direct = jnp.where(sub < 4, 0, 1) + 2 * c <= r
        for k in range(4):
            lower = acc_ref[pl.ds(pl.multiple_of(g * 32 + k * 8, 8), 8), :]
            m0 = acc_ref[pl.ds(pl.multiple_of(((2 * c) * 8 + r // 2) * 32 + k * 8, 8), 8), :]
            m1 = acc_ref[pl.ds(pl.multiple_of(((2 * c + 1) * 8 + r // 2) * 32 + k * 8, 8), 8), :]
            m0 = jnp.where(odd, pltpu.roll(m0, 4, axis=0), m0)
            m1 = jnp.where(odd, m1, pltpu.roll(m1, 4, axis=0))
            upper = jnp.where(sub < 4, m0, m1)
            block_ref[pl.ds(pl.multiple_of(g * 32 + k * 8, 8), 8), :] = jnp.where(direct, lower, upper)
        return 0

    lax.fori_loop(0, DEV, pack_device, 0)
    pltpu.make_async_copy(back_ref, back_ref, sem).wait()


def pack_back(acc):
    return pl.pallas_call(
        pack_kernel,
        out_shape=(array(DEV * BACK), array(DEV * BLOCK)),
        in_specs=[IN_VMEM],
        out_specs=(ANYWHERE, IN_VMEM),
        scratch_shapes=[pltpu.SemaphoreType.DMA],
        compiler_params=PARAMS,
        cost_estimate=cost(8),
        name="pack_back",
    )(acc)


def corner_kernel(where_ref, mine_ref, other_ref, l_ref, inv_ref, a_ref, s_ref):
    even = where_ref[1] % 2 == 0

    def load(halves):
        for (i, j), slot in corner_slot.items():
            a_ref[i * TILE : (i + 1) * TILE, j * TILE : (j + 1) * TILE] = halves[slot // HALF][
                pl.ds(slot % HALF, DEV, stride=HALF), :
            ]

    @pl.when(even)
    def _():
        load((mine_ref, other_ref))

    @pl.when(jnp.logical_not(even))
    def _():
        load((other_ref, mine_ref))

    l_ref[...] = jnp.zeros((PIV, PIV), jnp.float32)
    factor_blocks(a_ref, l_ref, inv_ref, s_ref, 0, PIV // TILE, PIV)


def factor_corner(where, mine, other):
    return pl.pallas_call(
        corner_kernel,
        out_shape=(array(PIV, PIV), array(PIV, WIDE)),
        in_specs=[IN_SMEM, IN_VMEM, IN_VMEM],
        out_specs=(IN_VMEM, IN_VMEM),
        scratch_shapes=[pltpu.VMEM((PIV, PIV), jnp.float32), pltpu.VMEM((SPREAD, TILE), jnp.float32)],
        compiler_params=PARAMS,
        cost_estimate=cost(50),
        name="corner",
    )(where, mine, other)


def panel_kernel(where_ref, in_ref, other_ref, l_ref, inv_ref, out_ref, x_ref, hi_ref, lo_ref):
    r = where_ref[0]
    c = where_ref[1]
    even = c % 2 == 0
    tile = lambda slot: in_ref[pl.ds(slot, DEV, stride=BACK), :]

    def load_rows(at, other_at):
        for a in range(2):
            for j in range(8):
                cols = slice(j * TILE, (j + 1) * TILE)
                x_ref[(at + a) * TILE : (at + a + 1) * TILE, cols] = tile(a * 8 + j)
                x_ref[(other_at + a) * TILE : (other_at + a + 1) * TILE, cols] = other_ref[
                    pl.ds(a * 8 + j, DEV, stride=16), :
                ]

    @pl.when(even)
    def _():
        load_rows(0, 2)

    @pl.when(jnp.logical_not(even))
    def _():
        load_rows(2, 0)

    @pl.when(r >= 2)
    def _():
        for a in range(8):
            for j in range(8):
                x_ref[PANEL + a * TILE : PANEL + (a + 1) * TILE, j * TILE : (j + 1) * TILE] = tile(16 + a * 8 + j)
        solve_rows(x_ref, hi_ref, lo_ref, l_ref, inv_ref, PIV)

    @pl.when((r >= 2) & (c >= 1))
    def _():
        out_ref[...] = dot_split(
            (hi_ref[:PANEL, :], lo_ref[:PANEL, :]), (hi_ref[PANEL:, :], lo_ref[PANEL:, :])
        )

    @pl.when((r >= 2) & (c == 0))
    def _():
        out_ref[...] = x_ref[:PANEL, :]

    @pl.when((r < 2) & (c == 0))
    def _():
        out_ref[...] = l_ref[pl.ds(pl.multiple_of(r * PANEL, PANEL), PANEL), :]

    @pl.when((r < 2) & (c >= 1))
    def _():
        out_ref[...] = jnp.zeros((PANEL, PIV), jnp.float32)


def solve_panel(where, arrived, other, corner, inverses):
    rows = 3 * PANEL
    return pl.pallas_call(
        panel_kernel,
        out_shape=array(PANEL, PIV),
        in_specs=[IN_SMEM] + [IN_VMEM] * 4,
        out_specs=IN_VMEM,
        scratch_shapes=[
            pltpu.VMEM((rows, PIV), jnp.float32),
            pltpu.VMEM((rows, PIV), jnp.bfloat16),
            pltpu.VMEM((rows, PIV), jnp.bfloat16),
        ],
        compiler_params=PARAMS,
        cost_estimate=cost(20),
        name="panel",
    )(where, arrived, other, corner, inverses)


def finish_kernel(where_ref, part_ref, in_ref, out_ref):
    r = where_ref[0]
    c = where_ref[1]
    trailing = (r >= 2) & (c >= 1)
    tile = lambda slot: in_ref[pl.ds(slot, DEV, stride=BLOCK), :]

    @pl.when(jnp.logical_not(trailing))
    def _():
        out_ref[...] = part_ref[...]

    @pl.when(trailing)
    def _():
        for q in range(2):
            for a in range(4):
                for b in range(4):
                    spot = (
                        slice(a * TILE, (a + 1) * TILE),
                        slice(q * PANEL + b * TILE, q * PANEL + (b + 1) * TILE),
                    )
                    mirrored = (r < 2 * c + q) | ((r == 2 * c + q) & (a < b))

                    @pl.when(mirrored)
                    def _():
                        out_ref[spot] = tile(b * 8 + q * 4 + a).T - part_ref[spot]

                    @pl.when(jnp.logical_not(mirrored))
                    def _():
                        out_ref[spot] = tile(a * 8 + q * 4 + b) - part_ref[spot]


def finish(where, part, arrived):
    return pl.pallas_call(
        finish_kernel,
        out_shape=array(PANEL, PIV),
        in_specs=[IN_SMEM, IN_VMEM, IN_VMEM],
        out_specs=IN_VMEM,
        compiler_params=pltpu.CompilerParams(vmem_limit_bytes=16 * 1024 * 1024),
        cost_estimate=cost(6),
        name="finish",
    )(where, part, arrived)


def exchange(x):
    y = x.reshape(DEV, x.shape[0] // DEV, TILE)
    return lax.all_to_all(y, AXES, 0, 0, tiled=True).reshape(x.shape)


def swap_cores(x):
    return lax.ppermute(x, "col", [(d, d ^ 1) for d in range(8)])


def on_device(child_fronts, child_tiles, parent_front):
    row = lax.axis_index("row")
    col = lax.axis_index("col")
    parent = parent_front.reshape(4, TILE, 8, TILE).transpose(1, 0, 2, 3).reshape(DEV * 32, TILE)
    parent = exchange(parent)
    tiles = jnp.pad(child_tiles.astype(jnp.float32), ((0, 7), (0, TILE - CT)))
    factor, outgoing = eliminate_child(child_fronts[0], tiles)
    outgoing, parent = lax.optimization_barrier((outgoing, parent))
    acc, corner_rows = sum_slices(parent, exchange(outgoing))
    where = jnp.stack([row, col]).astype(jnp.int32)
    panel_rows, block_rows = pack_back(acc)
    mine, panel_rows, block_rows = lax.optimization_barrier(
        (exchange(corner_rows), panel_rows, block_rows)
    )
    other = swap_cores(mine)
    corner, inverses = factor_corner(where, mine, other)
    arrived, corner, inverses = lax.optimization_barrier((exchange(panel_rows), corner, inverses))
    shared = arrived.reshape(DEV, BACK, TILE)[:, :16, :].reshape(DEV * 16, TILE)
    block_rows, arrived = lax.optimization_barrier((block_rows, arrived))
    part = solve_panel(where, arrived, swap_cores(shared), corner, inverses)
    result = finish(where, part, exchange(block_rows))
    return factor[None], result


def solution(mesh):
    placed = (P(AXES, None, None), P(AXES, None), P("row", "col"))
    return jax.shard_map(
        on_device,
        mesh=mesh,
        in_specs=placed,
        out_specs=(P(AXES, None, None), P("row", "col")),
        check_vma=False,
    )
```

```python
import functools

import jax
import jax.numpy as jnp
from jax import lax
from jax.experimental import pallas as pl
from jax.experimental.pallas import tpu as pltpu
from jax.sharding import PartitionSpec as P

PANEL = 512
TILE = 128
CP = 512
CW = 2048
CT = 12
REST = CW - CP
PIV = 1024
DEV = 128
PAIRS = CT * (CT + 1) // 2
AXES = ("row", "col")
PRECISE = lax.Precision.HIGHEST
VMEM = 61 * 1024 * 1024

SLOTS = 80
META = PAIRS
CHUNKS = 4

pair_slot = {}
for _i in range(CT):
    for _j in range(_i + 1):
        pair_slot[_i, _j] = len(pair_slot)

corner_slot = {}
for _i in range(8):
    for _j in range(_i + 1):
        corner_slot[_i, _j] = len(corner_slot)
HALF = 24
BACK = 80
BLOCK = 32
WIDE = 2 * TILE


def dot_t(x, y):
    return lax.dot_general(
        x, y, (((1,), (1,)), ((), ())), precision=PRECISE, preferred_element_type=jnp.float32
    )


def dot(x, y):
    return lax.dot_general(
        x, y, (((1,), (0,)), ((), ())), precision=PRECISE, preferred_element_type=jnp.float32
    )


def split(x):
    high = x.astype(jnp.bfloat16)
    return high, (x - high.astype(jnp.float32)).astype(jnp.bfloat16)


def dot_split(x, y):
    dims = (((1,), (1,)), ((), ()))
    f = functools.partial(lax.dot_general, dimension_numbers=dims, preferred_element_type=jnp.float32)
    return f(x[0], y[0]) + (f(x[0], y[1]) + f(x[1], y[0]))


def total(terms):
    while len(terms) > 1:
        terms = [terms[t] + terms[t + 1] for t in range(0, len(terms), 2)]
    return terms[0]


SPREAD = 256


def inverse_factor(tile, s_ref):
    shape = (8, TILE)
    lane = lax.broadcasted_iota(jnp.int32, shape, 1)
    sub = lax.broadcasted_iota(jnp.int32, shape, 0)
    column = lambda row, at: jnp.broadcast_to(row[:, at : at + 1], shape)
    spread = lambda at: s_ref[pl.ds(at, 8, stride=0), :]
    rows = [tile[8 * k : 8 * k + 8, :] for k in range(16)]
    out = []
    first = [column(rows[0], m) for m in range(8)]
    for k in range(16):
        base = 8 * k
        at = (k % 2) * 72
        columns = [first] + [[column(rows[q], base + m) for m in range(8)] for q in range(k + 1, 16)]
        if k < 15:
            first = [column(rows[k + 1], base + 8 + m) for m in range(8)]
        inside = (lane >= base) & (lane < base + 8)
        for m in range(8):
            s_ref[at + 8 * m : at + 8 * m + 8, :] = columns[0][m]
        s_ref[at + 64 : at + 72, :] = jnp.where(
            inside, jnp.where(lane - base == sub, 1.0, 0.0), rows[k]
        )
        v = [spread(at + 64 + m) for m in range(8)]
        a = [[spread(at + 8 * n + m) if n >= m else None for n in range(8)] for m in range(8)]
        w = []
        inverses = []
        for m in range(8):
            r = 1.0 / a[m][m]
            inverses.append(r)
            g = [a[m][n] * r if n > m else None for n in range(8)]
            for n in range(m + 1, 8):
                for p in range(n, 8):
                    a[n][p] = a[n][p] - g[n] * a[m][p]
            for n in range(m + 1, 8):
                v[n] = v[n] - g[n] * v[m]
            w.append(v[m] * r)
            for q in range(1, 16 - k):
                for n in range(m + 1, 8):
                    columns[q][n] = columns[q][n] - columns[q][m] * g[n]
        if k < 15:
            for m in range(8):
                s_ref[144 + 8 * m : 152 + 8 * m, :] = columns[1][m] * inverses[m]
            for n in range(8):
                first[n] = first[n] - total([columns[1][m] * spread(144 + 8 * m + n) for m in range(8)])
        for q in range(1, 16 - k):
            rows[k + q] = jnp.where(inside, 0.0, rows[k + q]) - total(
                [columns[q][m] * w[m] for m in range(8)]
            )
        mine, scale = v[0], a[0][0]
        for m in range(1, 8):
            mine = jnp.where(sub == m, v[m], mine)
            scale = jnp.where(sub == m, a[m][m], scale)
        out.append(jnp.where(lane <= base + sub, mine * lax.rsqrt(scale), 0.0))
    return jnp.concatenate(out, axis=0)


def factor_blocks(a_ref, l_ref, inv_ref, s_ref, first, last, order):
    count = order // TILE
    tri = lax.broadcasted_iota(jnp.int32, (TILE, TILE), 0) >= lax.broadcasted_iota(
        jnp.int32, (TILE, TILE), 1
    )

    def step(kb, _):
        at = pl.multiple_of(kb * TILE, TILE)
        inverse = inverse_factor(a_ref[pl.ds(at, TILE), pl.ds(at, TILE)], s_ref)
        inv_ref[pl.ds(at, TILE), pl.ds(pl.multiple_of((kb % 2) * TILE, TILE), TILE)] = inverse
        for q in range(first, last):

            @pl.when(kb == q)
            def _():
                lo = q * TILE
                half = q % 2 * TILE
                inverse = inv_ref[lo : lo + TILE, half : half + TILE]
                panel = dot_t(a_ref[lo:order, lo : lo + TILE], inverse)
                l_ref[lo : lo + TILE, lo : lo + TILE] = jnp.where(tri, panel[:TILE], 0.0)
                if q + 1 < count:
                    l_ref[lo + TILE : order, lo : lo + TILE] = panel[TILE:]
                    for j in range(q + 1, count):
                        left = panel[(j - q) * TILE :]
                        a_ref[j * TILE : order, j * TILE : (j + 1) * TILE] = a_ref[
                            j * TILE : order, j * TILE : (j + 1) * TILE
                        ] - dot_t(left, left[:TILE])
                if half:
                    up = inv_ref[lo - TILE : lo, :TILE]
                    inv_ref[lo - TILE : lo, TILE:] = jnp.zeros((TILE, TILE), jnp.float32)
                    inv_ref[lo : lo + TILE, :TILE] = -dot(
                        inverse, dot(l_ref[lo : lo + TILE, lo - TILE : lo], up)
                    )

        return 0

    lax.fori_loop(first, last, step, 0)


def solve_rows(x_ref, hi_ref, lo_ref, l_ref, inv_ref, order):
    for p in range(order // WIDE):
        lo = p * WIDE
        now = slice(lo, lo + WIDE)
        part = x_ref[:, now]
        if p:
            part = part - dot_split((hi_ref[:, :lo], lo_ref[:, :lo]), split(l_ref[now, :lo]))
        part = dot_split(split(part), split(inv_ref[now, :]))
        x_ref[:, now] = part
        hi_ref[:, now], lo_ref[:, now] = split(part)


def child_kernel(
    tiles_ref, front_ref, factor_out, rows_out,
    a_ref, b_ref, c_ref, inv_ref, s_ref, hi_ref, lo_ref, factor_ref, rows_ref, sems,
):
    copy_a = pltpu.make_async_copy(front_ref.at[pl.ds(0, CP), pl.ds(0, CP)], a_ref, sems.at[0])
    copy_b = pltpu.make_async_copy(front_ref.at[pl.ds(CP, REST), pl.ds(0, CP)], b_ref, sems.at[1])
    copy_c = pltpu.make_async_copy(front_ref.at[pl.ds(CP, REST), pl.ds(CP, REST)], c_ref, sems.at[2])
    copy_a.start()
    copy_b.start()
    copy_c.start()
    flat_ref = rows_ref.reshape(DEV * SLOTS, TILE)
    lane = lax.broadcasted_iota(jnp.int32, (DEV, TILE), 1)
    meta = jnp.zeros((DEV, TILE), jnp.int32)
    for t in range(CT):
        meta = jnp.where(lane == t, tiles_ref[0, t], meta)
    flat_ref[pl.ds(META, DEV, stride=SLOTS), :] = meta.astype(jnp.float32)
    flat_ref[pl.ds(META + 1, DEV, stride=SLOTS), :] = jnp.zeros((DEV, TILE), jnp.float32)
    factor_ref[...] = jnp.zeros((CP, CP), jnp.float32)
    copy_a.wait()
    factor_blocks(a_ref, factor_ref, inv_ref, s_ref, 0, CP // TILE, CP)
    send_corner = pltpu.make_async_copy(factor_ref, factor_out.at[pl.ds(0, CP)], sems.at[3])
    send_corner.start()
    copy_b.wait()
    solve_rows(b_ref, hi_ref, lo_ref, factor_ref, inv_ref, CP)
    send_below = pltpu.make_async_copy(b_ref, factor_out.at[pl.ds(CP, REST)], sems.at[4])
    send_below.start()
    copy_c.wait()
    sends = []
    for first in range(0, REST, WIDE):
        rows = slice(first, first + WIDE)
        wide = first + WIDE
        update = c_ref[rows, :wide] - dot_split(
            (hi_ref[rows, :], lo_ref[rows, :]), (hi_ref[:wide, :], lo_ref[:wide, :])
        )
        for k in range(2):
            i = first // TILE + k
            for j in range(i + 1):
                part = update[k * TILE : (k + 1) * TILE, j * TILE : (j + 1) * TILE]
                flat_ref[pl.ds(pair_slot[i, j], DEV, stride=SLOTS), :] = part
        done = SLOTS if wide == REST else (pair_slot[i, i] + 1) // 8 * 8
        sent = 8 * sum(groups for groups, _ in sends)
        if done > sent:
            copy = pltpu.make_async_copy(
                rows_ref.at[:, pl.ds(sent, done - sent)],
                rows_out.at[:, pl.ds(sent, done - sent)],
                sems.at[5 + len(sends)],
            )
            copy.start()
            sends.append(((done - sent) // 8, copy))
    send_corner.wait()
    send_below.wait()
    for _, copy in sends:
        copy.wait()


IN_VMEM = pl.BlockSpec(memory_space=pltpu.VMEM)
ANYWHERE = pl.BlockSpec(memory_space=pl.ANY)
IN_SMEM = pl.BlockSpec(memory_space=pltpu.SMEM)
PARAMS = pltpu.CompilerParams(vmem_limit_bytes=VMEM)


def cost(us):
    return pl.CostEstimate(flops=int(us * 10**9), bytes_accessed=int(us * 10**6), transcendentals=0)


def array(rows, columns=TILE, dtype=jnp.float32):
    return jax.ShapeDtypeStruct((rows, columns), dtype)


def eliminate_child(front, tiles):
    factor, rows = pl.pallas_call(
        child_kernel,
        out_shape=(array(CW, CP), jax.ShapeDtypeStruct((DEV, SLOTS, TILE), jnp.float32)),
        in_specs=[IN_SMEM, ANYWHERE],
        out_specs=(ANYWHERE, ANYWHERE),
        scratch_shapes=[
            pltpu.VMEM((CP, CP), jnp.float32),
            pltpu.VMEM((REST, CP), jnp.float32),
            pltpu.VMEM((REST, REST), jnp.float32),
            pltpu.VMEM((CP, WIDE), jnp.float32),
            pltpu.VMEM((SPREAD, TILE), jnp.float32),
            pltpu.VMEM((REST, CP), jnp.bfloat16),
            pltpu.VMEM((REST, CP), jnp.bfloat16),
            pltpu.VMEM((CP, CP), jnp.float32),
            pltpu.VMEM((DEV, SLOTS, TILE), jnp.float32),
            pltpu.SemaphoreType.DMA((5 + REST // WIDE,)),
        ],
        compiler_params=PARAMS,
        cost_estimate=cost(40),
        name="child",
    )(tiles, front)
    return factor, rows.reshape(DEV * SLOTS, TILE)


def sum_kernel(meta_in_ref, parent_ref, in_ref, acc_ref, corner_ref, rows_ref, half_ref, places_ref, pack_ref, table_ref, sems):
    piece = DEV * SLOTS // CHUNKS
    chunk = lambda k: pltpu.make_async_copy(
        in_ref.at[pl.ds(k * piece, piece)], rows_ref.at[pl.ds(k * piece, piece)], sems.at[k]
    )
    start = pltpu.make_async_copy(parent_ref, acc_ref, sems.at[CHUNKS])
    start.start()
    for k in range(CHUNKS):
        chunk(k).start()
    ids = meta_in_ref.reshape(DEV * 8, TILE)[pl.ds(META % 8, DEV, stride=8), :].astype(jnp.int32)
    half_ref[...] = jnp.zeros((DEV * 32, TILE), jnp.float32)
    as_row = (ids // 4) * 256 + (ids % 4) * 8
    as_col = (ids // 8) * 32 + ids % 8
    lane = lax.broadcasted_iota(jnp.int32, (DEV, TILE), 1)
    places_ref[...] = jnp.where(lane < 64, as_row, pltpu.roll(as_col, 64, axis=1))
    table = pltpu.make_async_copy(places_ref, table_ref, sems.at[CHUNKS + 1])
    table.start()
    table.wait()
    start.wait()
    todo = list(pair_slot.items())

    def add_children(p, _):
        pair = []
        for s, to_ref in ((2 * p, acc_ref), (2 * p + 1, half_ref)):
            row_of = [table_ref[s, i] for i in range(CT)]
            col_of = [table_ref[s, 64 + j] for j in range(CT)]
            pair.append((s * SLOTS, to_ref, row_of, col_of))
        for first in range(0, len(todo), 13):
            sums = []
            for base, to_ref, row_of, col_of in pair:
                for (i, j), slot in todo[first : first + 13]:
                    place = row_of[i] + col_of[j]
                    value = to_ref[pl.ds(place, 1), :] + rows_ref[pl.ds(base + slot, 1), :]
                    sums.append((to_ref, place, value))
            for to_ref, place, value in sums:
                to_ref[pl.ds(place, 1), :] = value
        return 0

    for k in range(CHUNKS):
        chunk(k).wait()
        lax.fori_loop(k * DEV // CHUNKS // 2, (k + 1) * DEV // CHUNKS // 2, add_children, 0)

    acc_ref[...] = acc_ref[...] + half_ref[...]
    for (i, j), slot in corner_slot.items():
        place = (i // 4) * 256 + (i % 4) * 8 + j
        pack_ref[slot : slot + 1, :] = acc_ref[place : place + 1, :]
    pack_ref[len(corner_slot) : 2 * HALF, :] = jnp.zeros((2 * HALF - len(corner_slot), TILE), jnp.float32)

    def send(g, _):
        pltpu.make_async_copy(
            pack_ref.at[pl.ds(pl.multiple_of((g % 2) * HALF, 8), HALF)],
            corner_ref.at[pl.ds(pl.multiple_of(g * HALF, 8), HALF)],
            sems.at[0],
        ).start()
        return 0

    lax.fori_loop(0, DEV, send, 0)
    pltpu.make_async_copy(corner_ref, corner_ref, sems.at[0]).wait()


def sum_slices(parent, arrived):
    return pl.pallas_call(
        sum_kernel,
        grid=(1,),
        out_shape=(array(DEV * 32), array(DEV * HALF)),
        in_specs=[pl.BlockSpec((DEV, 8, TILE), lambda i: (0, META // 8, 0)), ANYWHERE, ANYWHERE],
        out_specs=(IN_VMEM, ANYWHERE),
        scratch_shapes=[
            pltpu.VMEM((DEV * SLOTS, TILE), jnp.float32),
            pltpu.VMEM((DEV * 32, TILE), jnp.float32),
            pltpu.VMEM((DEV, TILE), jnp.int32),
            pltpu.VMEM((2 * HALF, TILE), jnp.float32),
            pltpu.SMEM((DEV, TILE), jnp.int32),
            pltpu.SemaphoreType.DMA((CHUNKS + 2,)),
        ],
        compiler_params=PARAMS,
        cost_estimate=cost(15),
        name="sum_slices",
    )(arrived.reshape(DEV, SLOTS, TILE), parent, arrived)


def pack_kernel(acc_ref, back_ref, block_ref, sem):
    sub = lax.broadcasted_iota(jnp.int32, (8, TILE), 0)

    def pack_device(g, _):
        r = g // 8
        c = g % 8
        base = pl.multiple_of(g * BACK, 8)
        for at, place, rows in (
            (0, r * 256 + (c % 2) * 16, 16),
            (16, c * 512, 32),
            (48, c * 512 + 256, 32),
        ):
            pltpu.make_async_copy(
                acc_ref.at[pl.ds(pl.multiple_of(place, 8), rows)],
                back_ref.at[pl.ds(pl.multiple_of(base + at, 8), rows)],
                sem,
            ).start()
        odd = (r % 2) == 1
        direct = jnp.where(sub < 4, 0, 1) + 2 * c <= r
        for k in range(4):
            lower = acc_ref[pl.ds(pl.multiple_of(g * 32 + k * 8, 8), 8), :]
            m0 = acc_ref[pl.ds(pl.multiple_of(((2 * c) * 8 + r // 2) * 32 + k * 8, 8), 8), :]
            m1 = acc_ref[pl.ds(pl.multiple_of(((2 * c + 1) * 8 + r // 2) * 32 + k * 8, 8), 8), :]
            m0 = jnp.where(odd, pltpu.roll(m0, 4, axis=0), m0)
            m1 = jnp.where(odd, m1, pltpu.roll(m1, 4, axis=0))
            upper = jnp.where(sub < 4, m0, m1)
            block_ref[pl.ds(pl.multiple_of(g * 32 + k * 8, 8), 8), :] = jnp.where(direct, lower, upper)
        return 0

    lax.fori_loop(0, DEV, pack_device, 0)
    pltpu.make_async_copy(back_ref, back_ref, sem).wait()


def pack_back(acc):
    return pl.pallas_call(
        pack_kernel,
        out_shape=(array(DEV * BACK), array(DEV * BLOCK)),
        in_specs=[IN_VMEM],
        out_specs=(ANYWHERE, IN_VMEM),
        scratch_shapes=[pltpu.SemaphoreType.DMA],
        compiler_params=PARAMS,
        cost_estimate=cost(8),
        name="pack_back",
    )(acc)


def corner_kernel(where_ref, mine_ref, other_ref, l_ref, inv_ref, a_ref, s_ref):
    even = where_ref[1] % 2 == 0

    def load(halves):
        for (i, j), slot in corner_slot.items():
            a_ref[i * TILE : (i + 1) * TILE, j * TILE : (j + 1) * TILE] = halves[slot // HALF][
                pl.ds(slot % HALF, DEV, stride=HALF), :
            ]

    @pl.when(even)
    def _():
        load((mine_ref, other_ref))

    @pl.when(jnp.logical_not(even))
    def _():
        load((other_ref, mine_ref))

    l_ref[...] = jnp.zeros((PIV, PIV), jnp.float32)
    factor_blocks(a_ref, l_ref, inv_ref, s_ref, 0, PIV // TILE, PIV)


def factor_corner(where, mine, other):
    return pl.pallas_call(
        corner_kernel,
        out_shape=(array(PIV, PIV), array(PIV, WIDE)),
        in_specs=[IN_SMEM, IN_VMEM, IN_VMEM],
        out_specs=(IN_VMEM, IN_VMEM),
        scratch_shapes=[pltpu.VMEM((PIV, PIV), jnp.float32), pltpu.VMEM((SPREAD, TILE), jnp.float32)],
        compiler_params=PARAMS,
        cost_estimate=cost(50),
        name="corner",
    )(where, mine, other)


def panel_kernel(where_ref, in_ref, other_ref, l_ref, inv_ref, out_ref, x_ref, hi_ref, lo_ref):
    r = where_ref[0]
    c = where_ref[1]
    even = c % 2 == 0
    tile = lambda slot: in_ref[pl.ds(slot, DEV, stride=BACK), :]

    def load_rows(at, other_at):
        for a in range(2):
            for j in range(8):
                cols = slice(j * TILE, (j + 1) * TILE)
                x_ref[(at + a) * TILE : (at + a + 1) * TILE, cols] = tile(a * 8 + j)
                x_ref[(other_at + a) * TILE : (other_at + a + 1) * TILE, cols] = other_ref[
                    pl.ds(a * 8 + j, DEV, stride=16), :
                ]

    @pl.when(even)
    def _():
        load_rows(0, 2)

    @pl.when(jnp.logical_not(even))
    def _():
        load_rows(2, 0)

    @pl.when(r >= 2)
    def _():
        for a in range(8):
            for j in range(8):
                x_ref[PANEL + a * TILE : PANEL + (a + 1) * TILE, j * TILE : (j + 1) * TILE] = tile(16 + a * 8 + j)
        solve_rows(x_ref, hi_ref, lo_ref, l_ref, inv_ref, PIV)

    @pl.when((r >= 2) & (c >= 1))
    def _():
        out_ref[...] = dot_split(
            (hi_ref[:PANEL, :], lo_ref[:PANEL, :]), (hi_ref[PANEL:, :], lo_ref[PANEL:, :])
        )

    @pl.when((r >= 2) & (c == 0))
    def _():
        out_ref[...] = x_ref[:PANEL, :]

    @pl.when((r < 2) & (c == 0))
    def _():
        out_ref[...] = l_ref[pl.ds(pl.multiple_of(r * PANEL, PANEL), PANEL), :]

    @pl.when((r < 2) & (c >= 1))
    def _():
        out_ref[...] = jnp.zeros((PANEL, PIV), jnp.float32)


def solve_panel(where, arrived, other, corner, inverses):
    rows = 3 * PANEL
    return pl.pallas_call(
        panel_kernel,
        out_shape=array(PANEL, PIV),
        in_specs=[IN_SMEM] + [IN_VMEM] * 4,
        out_specs=IN_VMEM,
        scratch_shapes=[
            pltpu.VMEM((rows, PIV), jnp.float32),
            pltpu.VMEM((rows, PIV), jnp.bfloat16),
            pltpu.VMEM((rows, PIV), jnp.bfloat16),
        ],
        compiler_params=PARAMS,
        cost_estimate=cost(20),
        name="panel",
    )(where, arrived, other, corner, inverses)


def finish_kernel(where_ref, part_ref, in_ref, out_ref):
    r = where_ref[0]
    c = where_ref[1]
    trailing = (r >= 2) & (c >= 1)
    tile = lambda slot: in_ref[pl.ds(slot, DEV, stride=BLOCK), :]

    @pl.when(jnp.logical_not(trailing))
    def _():
        out_ref[...] = part_ref[...]

    @pl.when(trailing)
    def _():
        for q in range(2):
            for a in range(4):
                for b in range(4):
                    spot = (
                        slice(a * TILE, (a + 1) * TILE),
                        slice(q * PANEL + b * TILE, q * PANEL + (b + 1) * TILE),
                    )
                    mirrored = (r < 2 * c + q) | ((r == 2 * c + q) & (a < b))

                    @pl.when(mirrored)
                    def _():
                        out_ref[spot] = tile(b * 8 + q * 4 + a).T - part_ref[spot]

                    @pl.when(jnp.logical_not(mirrored))
                    def _():
                        out_ref[spot] = tile(a * 8 + q * 4 + b) - part_ref[spot]


def finish(where, part, arrived):
    return pl.pallas_call(
        finish_kernel,
        out_shape=array(PANEL, PIV),
        in_specs=[IN_SMEM, IN_VMEM, IN_VMEM],
        out_specs=IN_VMEM,
        compiler_params=PARAMS,
        cost_estimate=cost(6),
        name="finish",
    )(where, part, arrived)


def exchange(x):
    y = x.reshape(DEV, x.shape[0] // DEV, TILE)
    return lax.all_to_all(y, AXES, 0, 0, tiled=True).reshape(x.shape)


def swap_cores(x):
    return lax.ppermute(x, "col", [(d, d ^ 1) for d in range(8)])


def on_device(child_fronts, child_tiles, parent_front):
    row = lax.axis_index("row")
    col = lax.axis_index("col")
    parent = parent_front.reshape(4, TILE, 8, TILE).transpose(1, 0, 2, 3).reshape(DEV * 32, TILE)
    parent = exchange(parent)
    factor, outgoing = eliminate_child(child_fronts[0], child_tiles)
    outgoing, parent = lax.optimization_barrier((outgoing, parent))
    acc, corner_rows = sum_slices(parent, exchange(outgoing))
    where = jnp.stack([row, col]).astype(jnp.int32)
    panel_rows, block_rows = pack_back(acc)
    mine, panel_rows, block_rows = lax.optimization_barrier(
        (exchange(corner_rows), panel_rows, block_rows)
    )
    other = swap_cores(mine)
    corner, inverses = factor_corner(where, mine, other)
    arrived, corner, inverses = lax.optimization_barrier((exchange(panel_rows), corner, inverses))
    shared = arrived.reshape(DEV, BACK, TILE)[:, :16, :].reshape(DEV * 16, TILE)
    block_rows, arrived = lax.optimization_barrier((block_rows, arrived))
    part = solve_panel(where, arrived, swap_cores(shared), corner, inverses)
    result = finish(where, part, exchange(block_rows))
    return factor[None], result


def solution(mesh):
    placed = (P(AXES, None, None), P(AXES, None), P("row", "col"))
    return jax.shard_map(
        on_device,
        mesh=mesh,
        in_specs=placed,
        out_specs=(P(AXES, None, None), P("row", "col")),
        check_vma=False,
    )
```
